256 devices in a mesh: seq: 64 (over z, y, x_lo), head: 4 (over x_hi, core).
Axes of the slice: x: 4 (x_hi: 2, x_lo: 2; x = x_hi * 2 + x_lo), y: 4, z: 8, core: 2. Of those that a mesh axis runs over, the one named last changes fastest.
Arguments:
- queries: float32 [8192, 8192], P('seq', 'head'), may hold values from -48 to 48
- prefix_keys: float32 [40960, 512], P('seq', 'head'), may hold values from -5 to 5
- prefix_value_rows: float32 [40960, 512], P('seq', 'head'), may hold values from -6 to 6
- response_keys: float32 [8192, 512], P('seq', 'head'), may hold values from -6 to 6
- response_values: float32 [8192, 512], P('seq', 'head'), may hold values from -6 to 6
- out_grad: float32 [8192, 8192], P('seq', 'head'), may hold values from -6 to 6
- lengths: int32 [64], P('seq'), may hold values from 32 to 128
Outputs:
- grad_queries: float32 [8192, 8192], P(('seq', 'head'))
- grad_prefix_keys: float32 [40960, 512], P('seq', 'head')
- grad_prefix_values: float32 [40960, 512], P('seq', 'head')
- grad_resp_keys: float32 [8192, 512], P('seq', 'head')
- grad_resp_values: float32 [8192, 512], P('seq', 'head')
The draws below stay inside these ranges and needn't reach their ends.
All inputs are finite; a program needn't handle non-finite values.
Results may differ from the reference program's by a relative error of at most 0.0003.
Values sent between devices are 32-bit elements; how exact they have to be, the bound alone decides.
No kernel may reach another device: no remote copies, remote signals or barrier semaphores. Data moves between devices by JAX's collectives and lax.ppermute only.
A program may use at most 128 MiB of HBM per device.

```python
import jax
import jax.numpy as jnp
from jax import lax

QUERY_HEAD_COUNT = 64
KEY_VALUE_HEADS = 4
HEAD_SIZE = 128
BLOCK_PREFIX = 640
R_DEV = 128
WINDOW = 3
PREFIX_TOKENS = 40960
RESPONSE_SLOTS = 8192
N_SEQ = 64


def joint_draw(key):
    random_key_for_keys = jax.random.fold_in(key, 101)
    key_query = jax.random.fold_in(key, 202)
    key_matrix = jnp.clip(jax.random.normal(random_key_for_keys, (N_SEQ, BLOCK_PREFIX, KEY_VALUE_HEADS, HEAD_SIZE), jnp.float32), -4.0, 4.0)
    query_matrix = jnp.clip(jax.random.normal(key_query, (N_SEQ, R_DEV, QUERY_HEAD_COUNT, HEAD_SIZE), jnp.float32), -4.0, 4.0)
    return (key_matrix.reshape(PREFIX_TOKENS, KEY_VALUE_HEADS * HEAD_SIZE), query_matrix.reshape(RESPONSE_SLOTS, QUERY_HEAD_COUNT * HEAD_SIZE))


def draw_queries(key, part):
    return joint_draw(key)[1]


def draw_prefix_keys(key, part):
    return joint_draw(key)[0]


def set_ends(entries, key, low, high):
    place = [jax.random.randint(jax.random.fold_in(key, axis), (), 0, length) for axis, length in enumerate(entries.shape)]
    longest = entries.shape.index(max(entries.shape))
    next_to = place[:longest] + [(place[longest] + 1) % entries.shape[longest]] + place[longest + 1:]
    return entries.at[tuple(place)].set(low).at[tuple(next_to)].set(high)


def shard_levels(stream_key, dims, pieces, low, high):
    def one(position, shards_of):
        draws = jax.random.uniform(jax.random.fold_in(jax.random.fold_in(stream_key, 6), position), (shards_of,), jnp.float32, low / len(pieces), high / len(pieces))
        return jnp.repeat(jnp.exp(draws), dims[position] // shards_of).reshape((-1,) + (1,) * (len(dims) - position - 1))

    factor_of = one(*pieces[0])
    for cut in pieces[1:]:
        factor_of = factor_of * one(*cut)
    return factor_of


def bell_draw(stream_key, dims, width, bound, split=(), held_as=jnp.bfloat16):
    entries = jax.random.normal(stream_key, dims, jnp.float32) * width
    if len(split) > 0:
        entries = shard_levels(stream_key, dims, split, -0.22, 0.18) * entries
    return jnp.clip(entries, min=-bound, max=bound).astype(held_as)


def setup_inputs(seed: int = 0) -> dict:
    key_of = jax.random.split(jax.random.key(seed), 8)
    return {
        "queries": draw_queries(jax.random.fold_in(key_of[7], 71), 0),
        "prefix_keys": draw_prefix_keys(jax.random.fold_in(key_of[7], 71), 0),
        "prefix_value_rows": bell_draw(key_of[2], (PREFIX_TOKENS, KEY_VALUE_HEADS * HEAD_SIZE), 1.0, 6.0, ((0, 64), (1, 4)), jnp.float32),
        "response_keys": bell_draw(key_of[3], (RESPONSE_SLOTS, KEY_VALUE_HEADS * HEAD_SIZE), 1.0, 6.0, ((0, 64), (1, 4)), jnp.float32),
        "response_values": bell_draw(key_of[4], (RESPONSE_SLOTS, KEY_VALUE_HEADS * HEAD_SIZE), 1.0, 6.0, ((0, 64), (1, 4)), jnp.float32),
        "out_grad": bell_draw(key_of[5], (RESPONSE_SLOTS, QUERY_HEAD_COUNT * HEAD_SIZE), 1.0, 6.0, ((0, 64), (1, 4)), jnp.float32),
        "lengths": set_ends(jax.random.randint(key_of[6], (N_SEQ,), max(4, R_DEV // 4), R_DEV + 1), jax.random.fold_in(key_of[6], 1), max(4, R_DEV // 4), R_DEV).astype(jnp.int32),
    }


def attend(query_row_block, visible_key_rows, visible_value_rows, local_block_keys, local_block_values, length):
    row_count = query_row_block.shape[0]
    group_size = QUERY_HEAD_COUNT // KEY_VALUE_HEADS
    prefix_length = visible_key_rows.shape[0]
    query_block = query_row_block.reshape(row_count, KEY_VALUE_HEADS, group_size, HEAD_SIZE)
    key_matrix = jnp.concatenate([visible_key_rows, local_block_keys], axis=0).reshape(prefix_length + row_count, KEY_VALUE_HEADS, HEAD_SIZE)
    value_matrix = jnp.concatenate([visible_value_rows, local_block_values], axis=0).reshape(prefix_length + row_count, KEY_VALUE_HEADS, HEAD_SIZE)
    scores = jnp.einsum('rkgd,skd->kgrs', query_block, key_matrix, precision=lax.Precision.HIGHEST) * HEAD_SIZE ** (-0.5)
    slot = jnp.arange(prefix_length + row_count, dtype=jnp.int32) - prefix_length
    token = jnp.arange(row_count, dtype=jnp.int32)
    visible = (slot[None, :] < 0) | (slot[None, :] <= token[:, None]) & (slot[None, :] < length)
    scores = jnp.where(visible[None, None], scores, -1e+30)
    probs = jax.nn.softmax(scores, axis=-1)
    result = jnp.einsum('kgrs,skd->rkgd', probs, value_matrix, precision=lax.Precision.HIGHEST)
    return result.reshape(row_count, QUERY_HEAD_COUNT * HEAD_SIZE)

def reference(queries, prefix_keys, prefix_value_rows, response_keys, response_values, out_grad, lengths):
    window_width = KEY_VALUE_HEADS * HEAD_SIZE
    q_blocks = queries.reshape(N_SEQ, R_DEV, QUERY_HEAD_COUNT * HEAD_SIZE)
    g_blocks = out_grad.reshape(N_SEQ, R_DEV, QUERY_HEAD_COUNT * HEAD_SIZE)
    kp_blocks = prefix_keys.reshape(N_SEQ, BLOCK_PREFIX, window_width)
    vp_blocks = prefix_value_rows.reshape(N_SEQ, BLOCK_PREFIX, window_width)
    kr_blocks = response_keys.reshape(N_SEQ, R_DEV, window_width)
    vr_blocks = response_values.reshape(N_SEQ, R_DEV, window_width)

    def one_response(index):
        picks = (index + jnp.arange(WINDOW, dtype=jnp.int32)) % N_SEQ
        visible_key_rows = jnp.take(kp_blocks, picks, axis=0).reshape(WINDOW * BLOCK_PREFIX, window_width)
        visible_value_rows = jnp.take(vp_blocks, picks, axis=0).reshape(WINDOW * BLOCK_PREFIX, window_width)
        length = lengths[index]
        valid = (jnp.arange(R_DEV, dtype=jnp.int32) < length).astype(jnp.float32)

        def forward(a, b, c, d, e):
            return attend(a, b, c, d, e, length)
        _, pullback = jax.vjp(forward, q_blocks[index], visible_key_rows, visible_value_rows, kr_blocks[index], vr_blocks[index])
        dq, dkw, dvw, dkr, dvr = pullback(g_blocks[index] * valid[:, None])
        return (dq, dkw.reshape(WINDOW, BLOCK_PREFIX, window_width), dvw.reshape(WINDOW, BLOCK_PREFIX, window_width), dkr, dvr)
    dq, dkw, dvw, dkr, dvr = lax.map(one_response, jnp.arange(N_SEQ, dtype=jnp.int32))
    grad_k = dkw[:, 0]
    grad_v = dvw[:, 0]
    for offset in range(1, WINDOW):
        grad_k = grad_k + jnp.roll(dkw[:, offset], offset, axis=0)
        grad_v = grad_v + jnp.roll(dvw[:, offset], offset, axis=0)
    return (dq.reshape(RESPONSE_SLOTS, QUERY_HEAD_COUNT * HEAD_SIZE), grad_k.reshape(PREFIX_TOKENS, window_width), grad_v.reshape(PREFIX_TOKENS, window_width), dkr.reshape(RESPONSE_SLOTS, window_width), dvr.reshape(RESPONSE_SLOTS, window_width))
```

```python
import jax
import jax.numpy as jnp
from jax import lax
from jax.experimental import pallas as pl
from jax.experimental.pallas import tpu as pltpu
from jax.sharding import PartitionSpec as P

HEAD_SIZE = 128
WINDOW = 3
LOG2E = 1.4426950408889634
F32, BF16 = jnp.float32, jnp.bfloat16
PAIR = 2


def passed_along(block, axis, distance):
    devices = range(lax.axis_size(axis))
    route = [((i - distance) % len(devices), i) for i in devices]
    return lax.ppermute(block, axis, route)


def parts_of(x):
    high = x.astype(BF16)
    return high, (x - high.astype(F32)).astype(BF16)


def nt(a, b):
    return lax.dot_general(a, b, (((1,), (1,)), ((), ())), preferred_element_type=F32)


def nn(a, b):
    return lax.dot_general(a, b, (((1,), (0,)), ((), ())), preferred_element_type=F32)


def attention_kernel(length_ref, q_ref, g_ref, *refs):
    nb = WINDOW + 1
    keys, values = refs[:nb], refs[nb : 2 * nb]
    dq_ref = refs[2 * nb]
    dk_refs, dv_refs = refs[2 * nb + 1 : 3 * nb + 1], refs[3 * nb + 1 : 4 * nb + 1]
    ka, va, kt, dk_sum, dv_sum = refs[4 * nb + 1 :]
    step = pl.program_id(0)
    rows = q_ref.shape[0]
    total = ka.shape[0]
    sizes = [k.shape[0] for k in keys]
    factor = HEAD_SIZE**-0.5

    @pl.when(step == 0)
    def _():
        at = 0
        for k_ref, v_ref, size in zip(keys, values, sizes):
            high, low = parts_of(k_ref[...])
            ka[at : at + size, :] = jnp.concatenate([high, low, high], axis=1)
            kt[:, at : at + size] = jnp.concatenate(
                [high.astype(F32).T, low.astype(F32).T], axis=0
            ).astype(BF16)
            high, low = parts_of(v_ref[...])
            va[at : at + size, :] = jnp.concatenate([high, low, high], axis=1)
            at += size
        dk_sum[...] = jnp.zeros_like(dk_sum)
        dv_sum[...] = jnp.zeros_like(dv_sum)

    length = length_ref[0]

    def stacked(ref):
        return jnp.concatenate(
            [ref[:, j * HEAD_SIZE : (j + 1) * HEAD_SIZE] for j in range(PAIR)], axis=0
        )

    q = stacked(q_ref) * (factor * LOG2E)
    token = lax.broadcasted_iota(jnp.int32, (PAIR, rows, HEAD_SIZE), 1).reshape(
        PAIR * rows, HEAD_SIZE
    )
    g = jnp.where(token < length, stacked(g_ref), 0.0)
    qh, ql = parts_of(q)
    gh, gl = parts_of(g)
    scores = nt(ka[...], jnp.concatenate([qh, qh, ql], axis=1))
    dprobs = nt(va[...], jnp.concatenate([gh, gh, gl], axis=1))
    slot = lax.broadcasted_iota(jnp.int32, (sizes[-1], PAIR * rows), 0)
    query = lax.broadcasted_iota(jnp.int32, (sizes[-1], PAIR * rows), 1) % rows
    visible = (slot <= query) & (slot < length)
    cut = total - sizes[-1]
    scores = jnp.concatenate(
        [scores[:cut], jnp.where(visible, scores[cut:], -1e30)], axis=0
    )
    top = jnp.max(scores, axis=0, keepdims=True)
    e = jnp.exp2(scores - top)
    inverse = 1.0 / jnp.sum(e, axis=0, keepdims=True)
    dsum = jnp.sum(e * dprobs, axis=0, keepdims=True) * inverse
    probs = e * inverse
    ds = probs * (dprobs - dsum)
    ph, plow = parts_of(probs)
    sh, sl = parts_of(ds)
    gg = jnp.concatenate([gh, gl], axis=1)
    qq = jnp.concatenate([qh, ql], axis=1)
    dv_sum[...] += nn(ph, gg) + nn(plow, gg)
    dk_sum[...] += nn(sh, qq) + nn(sl, qq)
    both = nn(kt[...], sh)
    dq_t = (both[:HEAD_SIZE] + both[HEAD_SIZE:] + nn(kt[:HEAD_SIZE], sl)) * factor
    dq = dq_t.T
    for j in range(PAIR):
        dq_ref[:, j * HEAD_SIZE : (j + 1) * HEAD_SIZE] = dq[j * rows : (j + 1) * rows]

    @pl.when(step == pl.num_programs(0) - 1)
    def _():
        at = 0
        for dk_ref, dv_ref, size in zip(dk_refs, dv_refs, sizes):
            here = slice(at, at + size)
            dk_ref[...] = (dk_sum[here, :HEAD_SIZE] + dk_sum[here, HEAD_SIZE:]) * (1.0 / LOG2E)
            dv_ref[...] = dv_sum[here, :HEAD_SIZE] + dv_sum[here, HEAD_SIZE:]
            at += size


def attention_grads(lengths, queries, out_grad, keys, values):
    rows, width = queries.shape
    total = sum(k.shape[0] for k in keys)
    chunk = PAIR * HEAD_SIZE
    per_head = pl.BlockSpec((rows, chunk), lambda i: (0, i))
    whole = [pl.BlockSpec(k.shape, lambda i: (0, 0)) for k in keys]
    like = [jax.ShapeDtypeStruct(k.shape, F32) for k in keys]
    return pl.pallas_call(
        attention_kernel,
        grid=(width // chunk,),
        in_specs=[pl.BlockSpec(memory_space=pltpu.SMEM), per_head, per_head] + whole + whole,
        out_specs=[per_head] + whole + whole,
        out_shape=[jax.ShapeDtypeStruct((rows, width), F32)] + like + like,
        scratch_shapes=[
            pltpu.VMEM((total, 3 * HEAD_SIZE), BF16),
            pltpu.VMEM((total, 3 * HEAD_SIZE), BF16),
            pltpu.VMEM((2 * HEAD_SIZE, total), BF16),
            pltpu.VMEM((total, 2 * HEAD_SIZE), F32),
            pltpu.VMEM((total, 2 * HEAD_SIZE), F32),
        ],
        compiler_params=pltpu.CompilerParams(vmem_limit_bytes=56 * 2**20),
        cost_estimate=pl.CostEstimate(
            flops=2 * 15 * rows * width * total, bytes_accessed=8_000_000, transcendentals=0
        ),
        name="attention_grads",
    )(lengths, queries, out_grad, *keys, *values)


def per_device(
    queries, prefix_keys, prefix_value_rows, response_keys, response_values, out_grad, lengths
):
    keys, values = [prefix_keys], [prefix_value_rows]
    for offset in range(1, WINDOW):
        keys.append(passed_along(prefix_keys, "seq", -offset))
        values.append(passed_along(prefix_value_rows, "seq", -offset))
    keys.append(response_keys)
    values.append(response_values)
    grads = attention_grads(lengths, queries, out_grad, keys, values)
    grad_query, dk, dv = grads[0], grads[1 : WINDOW + 2], grads[WINDOW + 2 :]
    grad_k, grad_v = dk[0], dv[0]
    for offset in range(1, WINDOW):
        grad_k = grad_k + passed_along(dk[offset], "seq", offset)
        grad_v = grad_v + passed_along(dv[offset], "seq", offset)
    grad_queries = lax.all_to_all(grad_query, "head", split_axis=0, concat_axis=1, tiled=True)
    return (grad_queries, grad_k, grad_v, dk[WINDOW], dv[WINDOW])


def solution(mesh):
    placed = (P("seq", "head"),) * 6 + (P("seq"),)
    return jax.shard_map(
        per_device,
        mesh=mesh,
        in_specs=placed,
        out_specs=(P(("seq", "head"), None),) + (P("seq", "head"),) * 4,
        check_vma=False,
    )
```

```python
import functools

import jax
import jax.numpy as jnp
from jax import lax
from jax.experimental import pallas as pl
from jax.experimental.pallas import tpu as pltpu
from jax.sharding import PartitionSpec as P

SIZE = 128
LOG2E = 1.4426950408889634
FACTOR = SIZE**-0.5
COST_CUT = 1
F32, BF16 = jnp.float32, jnp.bfloat16


def parts_of(x):
    high = x.astype(BF16)
    return high, (x - high.astype(F32)).astype(BF16)


def nt(a, b):
    return lax.dot_general(a, b, (((1,), (1,)), ((), ())), preferred_element_type=F32)


def nn(a, b):
    return lax.dot_general(a, b, (((1,), (0,)), ((), ())), preferred_element_type=F32)


def head_columns(head):
    return slice(head * SIZE, (head + 1) * SIZE)


def stacked(ref, first_head, pair):
    return jnp.concatenate([ref[:, head_columns(first_head + j)] for j in range(pair)], axis=0)


def load_rows(length, q_ref, g_ref, sub, pair):
    rows = q_ref.shape[0]
    q = stacked(q_ref, sub * pair, pair) * (FACTOR * LOG2E)
    token = lax.broadcasted_iota(jnp.int32, (pair, rows, SIZE), 1).reshape(pair * rows, SIZE)
    g = jnp.where(token < length, stacked(g_ref, sub * pair, pair), 0.0)
    return parts_of(q), parts_of(g)


def chunks_of(q_ref, pair):
    width = pair * q_ref.shape[0]
    for sub in range(q_ref.shape[1] // (pair * SIZE)):
        yield sub, slice(sub * width, (sub + 1) * width)


def keep_parts(refs, store):
    at = 0
    for ref in refs:
        high, low = parts_of(ref[...])
        store[at : at + ref.shape[0], :] = jnp.concatenate([high, low, high], axis=1)
        at += ref.shape[0]


def keep_turned(refs, store):
    at = 0
    for ref in refs:
        turned = ref[...].T
        high, low = parts_of(turned)
        store[:, at : at + ref.shape[0]] = jnp.concatenate([high, low], axis=0)
        at += ref.shape[0]


def masked(scores, length, rows, masked_rows):
    cut = scores.shape[0] - masked_rows
    slot = lax.broadcasted_iota(jnp.int32, (masked_rows, scores.shape[1]), 0)
    query = lax.broadcasted_iota(jnp.int32, (masked_rows, scores.shape[1]), 1) % rows
    visible = (slot <= query) & (slot < length)
    return jnp.concatenate([scores[:cut], jnp.where(visible, scores[cut:], -1e30)], axis=0)


def stats_rows(*rows):
    return jnp.concatenate(rows + (jnp.zeros((8 - len(rows), rows[0].shape[1]), F32),), axis=0)


def scores_and_dprobs(ka, va, rows):
    (qh, ql), (gh, gl) = rows
    scores = nt(ka[...], jnp.concatenate([qh, qh, ql], axis=1))
    dprobs = nt(va[...], jnp.concatenate([gh, gh, gl], axis=1))
    return scores, dprobs


def first_kernel(pair, key_count, count, masked_rows, length_ref, q_ref, g_ref, *refs):
    keys, values = refs[:key_count], refs[key_count:count]
    e_ref, dp_ref, stats_ref, ka, va = refs[count:]

    @pl.when(pl.program_id(0) == 0)
    def _():
        keep_parts(keys, ka)
        keep_parts(values, va)

    for sub, here in chunks_of(q_ref, pair):
        rows = load_rows(length_ref[0], q_ref, g_ref, sub, pair)
        scores, dprobs = scores_and_dprobs(ka, va, rows)
        if masked_rows:
            scores = masked(scores, length_ref[0], q_ref.shape[0], masked_rows)
        top = jnp.max(scores, axis=0, keepdims=True)
        e = jnp.exp2(scores - top)
        e_ref[:, here] = e
        dp_ref[:, here] = dprobs
        total = jnp.sum(e, axis=0, keepdims=True)
        weighted = jnp.sum(e * dprobs, axis=0, keepdims=True)
        stats_ref[:, here] = stats_rows(top, total, weighted)


def add_products(probs, ds, rows, kt, dk_sum, dv_sum):
    (qh, ql), (gh, gl) = rows
    ph, plow = parts_of(probs)
    sh, sl = parts_of(ds)
    gg = jnp.concatenate([gh, gl], axis=1)
    qq = jnp.concatenate([qh, ql], axis=1)
    dv_sum[...] += nn(jnp.concatenate([ph, plow], axis=1), jnp.concatenate([gg, gg], axis=0))
    dk_sum[...] += nn(jnp.concatenate([sh, sl], axis=1), jnp.concatenate([qq, qq], axis=0))
    both = nn(kt[...], sh)
    return ((both[:SIZE] + both[SIZE:] + nn(kt[:SIZE], sl)) * FACTOR).T


def store_query_grad(dq, before_ref, dq_ref, sub, pair):
    rows = dq_ref.shape[0]
    for j in range(pair):
        here = head_columns(sub * pair + j)
        part = dq[j * rows : (j + 1) * rows]
        dq_ref[:, here] = part if before_ref is None else part + before_ref[:, here]


def store_sums(refs, before, kept, scale):
    at = 0
    for j, ref in enumerate(refs):
        here = slice(at, at + ref.shape[0])
        part = (kept[here, :SIZE] + kept[here, SIZE:]) * scale
        ref[...] = part + before[j][...] if before else part
        at += ref.shape[0]


def start_sums(dk_sum, dv_sum):
    dk_sum[...] = jnp.zeros_like(dk_sum)
    dv_sum[...] = jnp.zeros_like(dv_sum)


def middle_kernel(pair, value_count, length_ref, q_ref, g_ref, stats_a, stats_b, k_ref, *refs):
    values = refs[:value_count]
    dq_ref, final_ref, dk_ref, dv_ref, ka, va, kt, dk_sum, dv_sum = refs[value_count:]

    @pl.when(pl.program_id(0) == 0)
    def _():
        keep_parts([k_ref], ka)
        keep_parts(values, va)
        keep_turned([k_ref], kt)
        start_sums(dk_sum, dv_sum)

    for sub, here in chunks_of(q_ref, pair):
        rows = load_rows(length_ref[0], q_ref, g_ref, sub, pair)
        scores, dprobs = scores_and_dprobs(ka, va, rows)
        top_a, top_b = stats_a[0:1, here], stats_b[0:1, here]
        top = jnp.maximum(jnp.maximum(top_a, top_b), jnp.max(scores, axis=0, keepdims=True))
        e = jnp.exp2(scores - top)
        fade_a, fade_b = jnp.exp2(top_a - top), jnp.exp2(top_b - top)
        total = stats_a[1:2, here] * fade_a + stats_b[1:2, here] * fade_b
        total = total + jnp.sum(e, axis=0, keepdims=True)
        weighted = stats_a[2:3, here] * fade_a + stats_b[2:3, here] * fade_b
        weighted = weighted + jnp.sum(e * dprobs, axis=0, keepdims=True)
        inverse = 1.0 / total
        dsum = weighted * inverse
        final_ref[:, here] = stats_rows(fade_a * inverse, fade_b * inverse, dsum)
        probs = e * inverse
        ds = probs * (dprobs - dsum)
        dq = add_products(probs, ds, rows, kt, dk_sum, dv_sum)
        store_query_grad(dq, None, dq_ref, sub, pair)

    @pl.when(pl.program_id(0) == pl.num_programs(0) - 1)
    def _():
        store_sums([dk_ref], [], dk_sum, 1.0 / LOG2E)
        store_sums([dv_ref], [], dv_sum, 1.0)


def last_kernel(
    pair, count, before_count, scale_row, pieces,
    length_ref, place_ref, q_ref, g_ref, before_ref, e_ref, dp_ref, final_ref, *refs,
):
    keys, refs = refs[:count], refs[count:]
    before_dk, before_dv = refs[:before_count], refs[before_count : 2 * before_count]
    refs = refs[2 * before_count :]
    dq_refs, refs = refs[:pieces], refs[pieces:]
    dk_refs, dv_refs = refs[:count], refs[count : 2 * count]
    kt, dk_sum, dv_sum, *held = refs[2 * count :]
    dq_ref = held[0] if held else dq_refs[0]

    @pl.when(pl.program_id(0) == 0)
    def _():
        keep_turned(keys, kt)
        start_sums(dk_sum, dv_sum)

    for sub, here in chunks_of(q_ref, pair):
        rows = load_rows(length_ref[0], q_ref, g_ref, sub, pair)
        probs = e_ref[:, here] * final_ref[scale_row : scale_row + 1, here]
        ds = probs * (dp_ref[:, here] - final_ref[2:3, here])
        dq = add_products(probs, ds, rows, kt, dk_sum, dv_sum)
        store_query_grad(dq, before_ref, dq_ref, sub, pair)
    if held:
        size = dq_ref.shape[0] // pieces
        for j in range(pieces):
            at = pl.multiple_of((place_ref[0] ^ j) * size, size)
            dq_refs[j][...] = dq_ref[pl.ds(at, size), :]

    @pl.when(pl.program_id(0) == pl.num_programs(0) - 1)
    def _():
        store_sums(dk_refs, before_dk, dk_sum, 1.0 / LOG2E)
        store_sums(dv_refs, before_dv, dv_sum, 1.0)


SMEM = pl.BlockSpec(memory_space=pltpu.SMEM)


def shape_of(*dims):
    return jax.ShapeDtypeStruct(dims, F32)


def by_columns(rows, width, first=0):
    return pl.BlockSpec((rows, width), lambda i: (0, i + first))


def whole(arrays):
    return [pl.BlockSpec(a.shape, lambda i: (0, 0)) for a in arrays]


def like(arrays):
    return [shape_of(*a.shape) for a in arrays]


def settings(products, rows, width, total, moved):
    return dict(
        compiler_params=pltpu.CompilerParams(vmem_limit_bytes=24 * 2**20),
        cost_estimate=pl.CostEstimate(
            flops=2 * products * 4 * rows * width * total // COST_CUT,
            bytes_accessed=moved // COST_CUT,
            transcendentals=0,
        ),
    )


def first_pass(lengths, queries, out_grad, keys, values, masked_rows, name, pair=8, step=8):
    rows, width = queries.shape
    total = sum(k.shape[0] for k in keys)
    slots = rows * width // SIZE
    per_head, per_slot = by_columns(rows, step * SIZE), by_columns(total, step * rows)
    return pl.pallas_call(
        functools.partial(first_kernel, pair, len(keys), len(keys) + len(values), masked_rows),
        grid=(width // (step * SIZE),),
        in_specs=[SMEM, per_head, per_head] + whole(keys) + whole(values),
        out_specs=[per_slot, per_slot, by_columns(8, step * rows)],
        out_shape=[shape_of(total, slots)] * 2 + [shape_of(8, slots)],
        scratch_shapes=[pltpu.VMEM((total, 3 * SIZE), BF16)] * 2,
        name=name,
        **settings(2, rows, width, total, 8 * total * slots),
    )(lengths, queries, out_grad, *keys, *values)


def middle_pass(lengths, queries, out_grad, stats_a, stats_b, key_block, values, pair=8, step=16):
    rows, width = queries.shape
    total = key_block.shape[0]
    slots = rows * width // SIZE
    per_head, stats = by_columns(rows, step * SIZE), by_columns(8, step * rows)
    return pl.pallas_call(
        functools.partial(middle_kernel, pair, len(values)),
        grid=(width // (step * SIZE),),
        in_specs=[SMEM, per_head, per_head, stats, stats] + whole([key_block]) + whole(values),
        out_specs=[per_head, stats] + whole([key_block, key_block]),
        out_shape=[shape_of(rows, width), shape_of(8, slots)] + like([key_block, key_block]),
        scratch_shapes=[pltpu.VMEM((total, 3 * SIZE), BF16)] * 2
        + [pltpu.VMEM((2 * SIZE, total), BF16)]
        + [pltpu.VMEM((total, 2 * SIZE), F32)] * 2,
        name="middle_pass",
        **settings(5, rows, width, total, 5_000_000),
    )(lengths, queries, out_grad, stats_a, stats_b, key_block, *values)


def last_pass(
    lengths, queries, out_grad, place, before, e, dp, final, scale_row, keys, name,
    first=0, heads=16, before_sums=(), pieces=1, pair=4, step=4,
):
    rows = queries.shape[0]
    total = sum(k.shape[0] for k in keys)
    start = first // step
    per_head = by_columns(rows, step * SIZE, start)
    per_slot = by_columns(total, step * rows, start)
    stats = by_columns(8, step * rows, start)
    return pl.pallas_call(
        functools.partial(last_kernel, pair, len(keys), len(before_sums) // 2, scale_row, pieces),
        grid=(heads // step,),
        in_specs=[SMEM, SMEM, per_head, per_head, per_head, per_slot, per_slot, stats]
        + whole(keys) + whole(before_sums),
        out_specs=[by_columns(rows // pieces, step * SIZE)] * pieces + whole(keys) + whole(keys),
        out_shape=[shape_of(rows // pieces, heads * SIZE)] * pieces + like(keys) + like(keys),
        scratch_shapes=[pltpu.VMEM((2 * SIZE, total), BF16)]
        + [pltpu.VMEM((total, 2 * SIZE), F32)] * 2
        + [pltpu.VMEM((rows, step * SIZE), F32)] * (pieces > 1),
        name=name,
        **settings(3, rows, heads * SIZE, total, 8 * total * heads * rows),
    )(lengths, place, queries, out_grad, before, e, dp, final, *keys, *before_sums)


def sum_kernel(odd_ref, own_ref, near_ref, far_ref, out_ref):
    near = jnp.where(odd_ref[0] == 1, near_ref[...], 0.0)
    out_ref[...] = own_ref[...] + near + far_ref[...]


def gather_kernel(count, place_ref, *refs):
    out_ref, half = refs[-1], refs[0].shape[1]
    for j in range(count):
        for k in range(2):
            at = pl.multiple_of(((place_ref[0] ^ j) * 2 + k) * half, half)
            out_ref[:, pl.ds(at, half)] = refs[2 * j + k][...]


def sum_pass(odd, own, near, far, name):
    blocks = whole([own, near, far])
    return pl.pallas_call(
        sum_kernel,
        grid=(1,),
        in_specs=[SMEM] + blocks,
        out_specs=blocks[0],
        out_shape=shape_of(*own.shape),
        name=name,
    )(odd, own, near, far)


def gather_pass(place, parts):
    rows, half = parts[0].shape
    return pl.pallas_call(
        functools.partial(gather_kernel, len(parts) // 2),
        grid=(1,),
        in_specs=[SMEM] + whole(parts),
        out_specs=pl.BlockSpec((rows, len(parts) * half), lambda i: (0, 0)),
        out_shape=shape_of(rows, len(parts) * half),
        name="gather_queries",
    )(place, *parts)


def per_device(
    queries, prefix_keys, prefix_value_rows, response_keys, response_values, out_grad, lengths
):
    count = lax.axis_size("seq")
    head_devices = lax.axis_size("head")
    even = lax.axis_index("seq") % 2 == 0
    odd = (lax.axis_index("seq") % 2).astype(jnp.int32).reshape(1)
    place = lax.axis_index("head").astype(jnp.int32).reshape(1)
    rows, width = queries.shape
    heads = width // SIZE
    half = prefix_keys.shape[0] // 2

    def from_two_on(block):
        return lax.ppermute(block, "seq", [((i + 2) % count, i) for i in range(count)])

    def to_two_on(block):
        return lax.ppermute(block, "seq", [(i, (i + 2) % count) for i in range(count)])

    def swapped(block):
        return lax.ppermute(block, "seq", [(i, i ^ 1) for i in range(count)])

    def exchanged(block, bits):
        return lax.ppermute(block, "head", [(i, i ^ bits) for i in range(head_devices)])

    def split_grads(grads):
        return grads[:head_devices], grads[head_devices:]

    args = (lengths, queries, out_grad)
    value_parts = [prefix_value_rows[:half], prefix_value_rows[half:]]
    far_k = from_two_on(prefix_keys)
    far_v = [from_two_on(part) for part in value_parts]

    own_keys, own_values = [prefix_keys, response_keys], [prefix_value_rows, response_values]
    own_e, own_dp, own_stats = first_pass(*args, own_keys, own_values, rows, "own_scores")
    own_stats, far_k = lax.optimization_barrier((own_stats, far_k))
    near_k = swapped(jnp.where(even, far_k, prefix_keys))
    near_v = []
    for j in range(2):
        own_stats, far_v[j] = lax.optimization_barrier((own_stats, far_v[j]))
        chosen = jnp.where(even, far_v[j], value_parts[j])
        near_v.append(swapped(chosen))
    own_stats, far_k, chosen = lax.optimization_barrier((own_stats, far_k, chosen))
    far_e, far_dp, far_stats = first_pass(*args, [far_k], far_v, 0, "far_scores")
    near_dq, final, near_dk, near_dv = middle_pass(*args, own_stats, far_stats, near_k, near_v)

    from_near_dv, from_near_dk = swapped(near_dv), swapped(near_dk)
    far_dq, far_dk, far_dv = last_pass(
        *args, place, near_dq, far_e, far_dp, final, 1, [far_k], "far_grads"
    )
    to_far_dv = far_dv + jnp.where(even, from_near_dv, 0.0)
    from_far_dv = to_two_on(to_far_dv)
    far_dq, to_far_dv = lax.optimization_barrier((far_dq, to_far_dv))
    dq_a, sums = split_grads(last_pass(
        *args, place, far_dq, own_e, own_dp, final, 0, own_keys, "own_grads_a",
        first=0, heads=heads // 2, pieces=head_devices,
    ))
    got_a = [dq_a[0]] + [exchanged(dq_a[j], j) for j in range(1, head_devices)]
    to_far_dk = far_dk + jnp.where(even, from_near_dk, 0.0)
    sums, to_far_dk, far_dq = lax.optimization_barrier((sums, to_far_dk, far_dq))
    from_far_dk = to_two_on(to_far_dk)
    dq_b, (own_dk, resp_dk, own_dv, resp_dv) = split_grads(last_pass(
        *args, place, far_dq, own_e, own_dp, final, 0, own_keys, "own_grads_b",
        first=heads // 2, heads=heads // 2, before_sums=sums, pieces=head_devices,
    ))
    got_a, dq_b = lax.optimization_barrier((got_a, dq_b))
    got_b = [dq_b[0]] + [exchanged(dq_b[j], j) for j in range(1, head_devices)]
    grad_v = sum_pass(odd, own_dv, from_near_dv, from_far_dv, "sum_values")
    grad_k = sum_pass(odd, own_dk, from_near_dk, from_far_dk, "sum_keys")
    got_b, grad_k, grad_v = lax.optimization_barrier((got_b, grad_k, grad_v))
    grad_queries = gather_pass(place, [x for pair in zip(got_a, got_b) for x in pair])
    return (grad_queries, grad_k, grad_v, resp_dk, resp_dv)


def solution(mesh):
    placed = (P("seq", "head"),) * 6 + (P("seq"),)
    return jax.shard_map(
        per_device,
        mesh=mesh,
        in_specs=placed,
        out_specs=(P(("seq", "head"), None),) + (P("seq", "head"),) * 4,
        check_vma=False,
    )
```

```python
import functools

import jax
import jax.numpy as jnp
from jax import lax
from jax.experimental import pallas as pl
from jax.experimental.pallas import tpu as pltpu
from jax.sharding import PartitionSpec as P

SIZE = 128
LOG2E = 1.4426950408889634
FACTOR = SIZE**-0.5
COST_CUT = 1
F32, BF16 = jnp.float32, jnp.bfloat16


def parts_of(x):
    high = x.astype(BF16)
    return high, (x - high.astype(F32)).astype(BF16)


def nt(a, b):
    return lax.dot_general(a, b, (((1,), (1,)), ((), ())), preferred_element_type=F32)


def nn(a, b):
    return lax.dot_general(a, b, (((1,), (0,)), ((), ())), preferred_element_type=F32)


def head_columns(head):
    return slice(head * SIZE, (head + 1) * SIZE)


def stacked(ref, first_head, pair):
    return jnp.concatenate([ref[:, head_columns(first_head + j)] for j in range(pair)], axis=0)


def load_rows(length, q_ref, g_ref, sub, pair):
    rows = q_ref.shape[0]
    q = stacked(q_ref, sub * pair, pair) * (FACTOR * LOG2E)
    token = lax.broadcasted_iota(jnp.int32, (pair, rows, SIZE), 1).reshape(pair * rows, SIZE)
    g = jnp.where(token < length, stacked(g_ref, sub * pair, pair), 0.0)
    return parts_of(q), parts_of(g)


def chunks_of(q_ref, pair):
    width = pair * q_ref.shape[0]
    for sub in range(q_ref.shape[1] // (pair * SIZE)):
        yield sub, slice(sub * width, (sub + 1) * width)


def keep_parts(refs, store):
    at = 0
    for ref in refs:
        high, low = parts_of(ref[...])
        store[at : at + ref.shape[0], :] = jnp.concatenate([high, low, high], axis=1)
        at += ref.shape[0]


def keep_turned(refs, store):
    at = 0
    for ref in refs:
        turned = ref[...].T
        high, low = parts_of(turned)
        store[:, at : at + ref.shape[0]] = jnp.concatenate([high, low], axis=0)
        at += ref.shape[0]


def masked(scores, length, rows, masked_rows):
    cut = scores.shape[0] - masked_rows
    slot = lax.broadcasted_iota(jnp.int32, (masked_rows, scores.shape[1]), 0)
    query = lax.broadcasted_iota(jnp.int32, (masked_rows, scores.shape[1]), 1) % rows
    visible = (slot <= query) & (slot < length)
    return jnp.concatenate([scores[:cut], jnp.where(visible, scores[cut:], -1e30)], axis=0)


def stats_rows(*rows):
    return jnp.concatenate(rows + (jnp.zeros((8 - len(rows), rows[0].shape[1]), F32),), axis=0)


def scores_and_dprobs(ka, va, rows):
    (qh, ql), (gh, gl) = rows
    scores = nt(ka[...], jnp.concatenate([qh, qh, ql], axis=1))
    dprobs = nt(va[...], jnp.concatenate([gh, gh, gl], axis=1))
    return scores, dprobs


def first_kernel(pair, key_count, count, masked_rows, length_ref, q_ref, g_ref, *refs):
    keys, values = refs[:key_count], refs[key_count:count]
    e_ref, dp_ref, stats_ref, ka, va = refs[count:]

    @pl.when(pl.program_id(0) == 0)
    def _():
        keep_parts(keys, ka)
        keep_parts(values, va)

    for sub, here in chunks_of(q_ref, pair):
        rows = load_rows(length_ref[0], q_ref, g_ref, sub, pair)
        scores, dprobs = scores_and_dprobs(ka, va, rows)
        if masked_rows:
            scores = masked(scores, length_ref[0], q_ref.shape[0], masked_rows)
        top = jnp.max(scores, axis=0, keepdims=True)
        e = jnp.exp2(scores - top)
        e_ref[:, here] = e
        dp_ref[:, here] = dprobs
        total = jnp.sum(e, axis=0, keepdims=True)
        weighted = jnp.sum(e * dprobs, axis=0, keepdims=True)
        stats_ref[:, here] = stats_rows(top, total, weighted)


def add_products(probs, ds, rows, kt, dk_sum, dv_sum):
    (qh, ql), (gh, gl) = rows
    ph, plow = parts_of(probs)
    sh, sl = parts_of(ds)
    gg = jnp.concatenate([gh, gl], axis=1)
    qq = jnp.concatenate([qh, ql], axis=1)
    dv_sum[...] += nn(jnp.concatenate([ph, plow], axis=1), jnp.concatenate([gg, gg], axis=0))
    dk_sum[...] += nn(jnp.concatenate([sh, sl], axis=1), jnp.concatenate([qq, qq], axis=0))
    both = nn(kt[...], sh)
    return ((both[:SIZE] + both[SIZE:] + nn(kt[:SIZE], sl)) * FACTOR).T


def store_query_grad(dq, before_ref, dq_ref, sub, pair):
    rows = dq_ref.shape[0]
    for j in range(pair):
        here = head_columns(sub * pair + j)
        part = dq[j * rows : (j + 1) * rows]
        dq_ref[:, here] = part if before_ref is None else part + before_ref[:, here]


def store_sums(refs, before, kept, scale):
    at = 0
    for j, ref in enumerate(refs):
        here = slice(at, at + ref.shape[0])
        part = (kept[here, :SIZE] + kept[here, SIZE:]) * scale
        ref[...] = part + before[j][...] if before else part
        at += ref.shape[0]


def start_sums(dk_sum, dv_sum):
    dk_sum[...] = jnp.zeros_like(dk_sum)
    dv_sum[...] = jnp.zeros_like(dv_sum)


def middle_kernel(pair, value_count, length_ref, q_ref, g_ref, stats_a, stats_b, k_ref, *refs):
    values = refs[:value_count]
    dq_ref, final_ref, dk_ref, dv_ref, ka, va, kt, dk_sum, dv_sum = refs[value_count:]

    @pl.when(pl.program_id(0) == 0)
    def _():
        keep_parts([k_ref], ka)
        keep_parts(values, va)
        keep_turned([k_ref], kt)
        start_sums(dk_sum, dv_sum)

    for sub, here in chunks_of(q_ref, pair):
        rows = load_rows(length_ref[0], q_ref, g_ref, sub, pair)
        scores, dprobs = scores_and_dprobs(ka, va, rows)
        top_a, top_b = stats_a[0:1, here], stats_b[0:1, here]
        top = jnp.maximum(jnp.maximum(top_a, top_b), jnp.max(scores, axis=0, keepdims=True))
        e = jnp.exp2(scores - top)
        fade_a, fade_b = jnp.exp2(top_a - top), jnp.exp2(top_b - top)
        total = stats_a[1:2, here] * fade_a + stats_b[1:2, here] * fade_b
        total = total + jnp.sum(e, axis=0, keepdims=True)
        weighted = stats_a[2:3, here] * fade_a + stats_b[2:3, here] * fade_b
        weighted = weighted + jnp.sum(e * dprobs, axis=0, keepdims=True)
        inverse = 1.0 / total
        dsum = weighted * inverse
        final_ref[:, here] = stats_rows(fade_a * inverse, fade_b * inverse, dsum)
        probs = e * inverse
        ds = probs * (dprobs - dsum)
        dq = add_products(probs, ds, rows, kt, dk_sum, dv_sum)
        store_query_grad(dq, None, dq_ref, sub, pair)

    @pl.when(pl.program_id(0) == pl.num_programs(0) - 1)
    def _():
        store_sums([dk_ref], [], dk_sum, 1.0 / LOG2E)
        store_sums([dv_ref], [], dv_sum, 1.0)


def last_kernel(
    pair, count, before_count, scale_row, pieces,
    length_ref, place_ref, q_ref, g_ref, before_ref, e_ref, dp_ref, final_ref, *refs,
):
    keys, refs = refs[:count], refs[count:]
    before_dk, before_dv = refs[:before_count], refs[before_count : 2 * before_count]
    refs = refs[2 * before_count :]
    dq_refs, refs = refs[:pieces], refs[pieces:]
    dk_refs, dv_refs = refs[:count], refs[count : 2 * count]
    kt, dk_sum, dv_sum, *held = refs[2 * count :]
    dq_ref = held[0] if held else dq_refs[0]

    @pl.when(pl.program_id(0) == 0)
    def _():
        keep_turned(keys, kt)
        start_sums(dk_sum, dv_sum)

    for sub, here in chunks_of(q_ref, pair):
        rows = load_rows(length_ref[0], q_ref, g_ref, sub, pair)
        probs = e_ref[:, here] * final_ref[scale_row : scale_row + 1, here]
        ds = probs * (dp_ref[:, here] - final_ref[2:3, here])
        dq = add_products(probs, ds, rows, kt, dk_sum, dv_sum)
        store_query_grad(dq, before_ref, dq_ref, sub, pair)
    if held:
        size = dq_ref.shape[0] // pieces
        for j in range(pieces):
            at = pl.multiple_of((place_ref[0] ^ j) * size, size)
            dq_refs[j][...] = dq_ref[pl.ds(at, size), :]

    @pl.when(pl.program_id(0) == pl.num_programs(0) - 1)
    def _():
        store_sums(dk_refs, before_dk, dk_sum, 1.0 / LOG2E)
        store_sums(dv_refs, before_dv, dv_sum, 1.0)


SMEM = pl.BlockSpec(memory_space=pltpu.SMEM)


def shape_of(*dims):
    return jax.ShapeDtypeStruct(dims, F32)


def by_columns(rows, width, first=0):
    return pl.BlockSpec((rows, width), lambda i: (0, i + first))


def whole(arrays):
    return [pl.BlockSpec(a.shape, lambda i: (0, 0)) for a in arrays]


def like(arrays):
    return [shape_of(*a.shape) for a in arrays]


def settings(products, rows, width, total, moved):
    return dict(
        compiler_params=pltpu.CompilerParams(vmem_limit_bytes=24 * 2**20),
        cost_estimate=pl.CostEstimate(
            flops=2 * products * 4 * rows * width * total // COST_CUT,
            bytes_accessed=moved // COST_CUT,
            transcendentals=0,
        ),
    )


def first_pass(lengths, queries, out_grad, keys, values, masked_rows, name, pair=8, step=8):
    rows, width = queries.shape
    total = sum(k.shape[0] for k in keys)
    slots = rows * width // SIZE
    per_head, per_slot = by_columns(rows, step * SIZE), by_columns(total, step * rows)
    return pl.pallas_call(
        functools.partial(first_kernel, pair, len(keys), len(keys) + len(values), masked_rows),
        grid=(width // (step * SIZE),),
        in_specs=[SMEM, per_head, per_head] + whole(keys) + whole(values),
        out_specs=[per_slot, per_slot, by_columns(8, step * rows)],
        out_shape=[shape_of(total, slots)] * 2 + [shape_of(8, slots)],
        scratch_shapes=[pltpu.VMEM((total, 3 * SIZE), BF16)] * 2,
        name=name,
        **settings(2, rows, width, total, 8 * total * slots),
    )(lengths, queries, out_grad, *keys, *values)


def middle_pass(lengths, queries, out_grad, stats_a, stats_b, key_block, values, pair=8, step=16):
    rows, width = queries.shape
    total = key_block.shape[0]
    slots = rows * width // SIZE
    per_head, stats = by_columns(rows, step * SIZE), by_columns(8, step * rows)
    return pl.pallas_call(
        functools.partial(middle_kernel, pair, len(values)),
        grid=(width // (step * SIZE),),
        in_specs=[SMEM, per_head, per_head, stats, stats] + whole([key_block]) + whole(values),
        out_specs=[per_head, stats] + whole([key_block, key_block]),
        out_shape=[shape_of(rows, width), shape_of(8, slots)] + like([key_block, key_block]),
        scratch_shapes=[pltpu.VMEM((total, 3 * SIZE), BF16)] * 2
        + [pltpu.VMEM((2 * SIZE, total), BF16)]
        + [pltpu.VMEM((total, 2 * SIZE), F32)] * 2,
        name="middle_pass",
        **settings(5, rows, width, total, 5_000_000),
    )(lengths, queries, out_grad, stats_a, stats_b, key_block, *values)


def last_pass(
    lengths, queries, out_grad, place, before, e, dp, final, scale_row, keys, name,
    first=0, heads=16, before_sums=(), pieces=1, pair=4, step=4,
):
    rows = queries.shape[0]
    total = sum(k.shape[0] for k in keys)
    start = first // step
    per_head = by_columns(rows, step * SIZE, start)
    per_slot = by_columns(total, step * rows, start)
    stats = by_columns(8, step * rows, start)
    return pl.pallas_call(
        functools.partial(last_kernel, pair, len(keys), len(before_sums) // 2, scale_row, pieces),
        grid=(heads // step,),
        in_specs=[SMEM, SMEM, per_head, per_head, per_head, per_slot, per_slot, stats]
        + whole(keys) + whole(before_sums),
        out_specs=[by_columns(rows // pieces, step * SIZE)] * pieces + whole(keys) + whole(keys),
        out_shape=[shape_of(rows // pieces, heads * SIZE)] * pieces + like(keys) + like(keys),
        scratch_shapes=[pltpu.VMEM((2 * SIZE, total), BF16)]
        + [pltpu.VMEM((total, 2 * SIZE), F32)] * 2
        + [pltpu.VMEM((rows, step * SIZE), F32)] * (pieces > 1),
        name=name,
        **settings(3, rows, heads * SIZE, total, 8 * total * heads * rows),
    )(lengths, place, queries, out_grad, before, e, dp, final, *keys, *before_sums)


def sum_kernel(odd_ref, own_ref, near_ref, far_ref, out_ref):
    near = jnp.where(odd_ref[0] == 1, near_ref[...], 0.0)
    out_ref[...] = own_ref[...] + near + far_ref[...]


def gather_kernel(count, place_ref, *refs):
    out_ref, half = refs[-1], refs[0].shape[1]
    for j in range(count):
        for k in range(2):
            at = pl.multiple_of(((place_ref[0] ^ j) * 2 + k) * half, half)
            out_ref[:, pl.ds(at, half)] = refs[2 * j + k][...]


def sum_pass(odd, own, near, far, name):
    blocks = whole([own, near, far])
    return pl.pallas_call(
        sum_kernel,
        grid=(1,),
        in_specs=[SMEM] + blocks,
        out_specs=blocks[0],
        out_shape=shape_of(*own.shape),
        compiler_params=pltpu.CompilerParams(vmem_limit_bytes=8 * 2**20),
        name=name,
    )(odd, own, near, far)


def gather_pass(place, parts):
    rows, half = parts[0].shape
    return pl.pallas_call(
        functools.partial(gather_kernel, len(parts) // 2),
        grid=(1,),
        in_specs=[SMEM] + whole(parts),
        out_specs=pl.BlockSpec((rows, len(parts) * half), lambda i: (0, 0)),
        out_shape=shape_of(rows, len(parts) * half),
        compiler_params=pltpu.CompilerParams(vmem_limit_bytes=8 * 2**20),
        name="gather_queries",
    )(place, *parts)


def per_device(
    queries, prefix_keys, prefix_value_rows, response_keys, response_values, out_grad, lengths
):
    count = lax.axis_size("seq")
    head_devices = lax.axis_size("head")
    even = lax.axis_index("seq") % 2 == 0
    odd = (lax.axis_index("seq") % 2).astype(jnp.int32).reshape(1)
    place = lax.axis_index("head").astype(jnp.int32).reshape(1)
    rows, width = queries.shape
    heads = width // SIZE
    half = prefix_keys.shape[0] // 2

    def from_two_on(block):
        return lax.ppermute(block, "seq", [((i + 2) % count, i) for i in range(count)])

    def to_two_on(block):
        return lax.ppermute(block, "seq", [(i, (i + 2) % count) for i in range(count)])

    def swapped(block):
        return lax.ppermute(block, "seq", [(i, i ^ 1) for i in range(count)])

    def exchanged(block, bits):
        return lax.ppermute(block, "head", [(i, i ^ bits) for i in range(head_devices)])

    def split_grads(grads):
        return grads[:head_devices], grads[head_devices:]

    args = (lengths, queries, out_grad)
    value_parts = [prefix_value_rows[:half], prefix_value_rows[half:]]
    far_k = from_two_on(prefix_keys)
    far_v = [from_two_on(part) for part in value_parts]

    own_keys, own_values = [prefix_keys, response_keys], [prefix_value_rows, response_values]
    own_e, own_dp, own_stats = first_pass(*args, own_keys, own_values, rows, "own_scores")
    own_stats, far_k = lax.optimization_barrier((own_stats, far_k))
    near_k = swapped(jnp.where(even, far_k, prefix_keys))
    near_v = []
    for j in range(2):
        own_stats, far_v[j] = lax.optimization_barrier((own_stats, far_v[j]))
        chosen = jnp.where(even, far_v[j], value_parts[j])
        near_v.append(swapped(chosen))
    own_stats, far_k, chosen = lax.optimization_barrier((own_stats, far_k, chosen))
    far_e, far_dp, far_stats = first_pass(*args, [far_k], far_v, 0, "far_scores")
    near_dq, final, near_dk, near_dv = middle_pass(*args, own_stats, far_stats, near_k, near_v)

    from_near_dv, from_near_dk = swapped(near_dv), swapped(near_dk)
    far_dq, far_dk, far_dv = last_pass(
        *args, place, near_dq, far_e, far_dp, final, 1, [far_k], "far_grads"
    )
    to_far_dv = far_dv + jnp.where(even, from_near_dv, 0.0)
    from_far_dv = to_two_on(to_far_dv)
    far_dq, to_far_dv = lax.optimization_barrier((far_dq, to_far_dv))
    dq_a, sums = split_grads(last_pass(
        *args, place, far_dq, own_e, own_dp, final, 0, own_keys, "own_grads_a",
        first=0, heads=heads // 2, pieces=head_devices,
    ))
    got_a = [dq_a[0]] + [exchanged(dq_a[j], j) for j in range(1, head_devices)]
    to_far_dk = far_dk + jnp.where(even, from_near_dk, 0.0)
    sums, to_far_dk, far_dq = lax.optimization_barrier((sums, to_far_dk, far_dq))
    from_far_dk = to_two_on(to_far_dk)
    dq_b, (own_dk, resp_dk, own_dv, resp_dv) = split_grads(last_pass(
        *args, place, far_dq, own_e, own_dp, final, 0, own_keys, "own_grads_b",
        first=heads // 2, heads=heads // 2, before_sums=sums, pieces=head_devices,
    ))
    got_a, dq_b = lax.optimization_barrier((got_a, dq_b))
    got_b = [dq_b[0]] + [exchanged(dq_b[j], j) for j in range(1, head_devices)]
    grad_v = sum_pass(odd, own_dv, from_near_dv, from_far_dv, "sum_values")
    grad_k = sum_pass(odd, own_dk, from_near_dk, from_far_dk, "sum_keys")
    got_b, grad_k, grad_v = lax.optimization_barrier((got_b, grad_k, grad_v))
    grad_queries = gather_pass(place, [x for pair in zip(got_a, got_b) for x in pair])
    return (grad_queries, grad_k, grad_v, resp_dk, resp_dv)


def solution(mesh):
    placed = (P("seq", "head"),) * 6 + (P("seq"),)
    return jax.shard_map(
        per_device,
        mesh=mesh,
        in_specs=placed,
        out_specs=(P(("seq", "head"), None),) + (P("seq", "head"),) * 4,
        check_vma=False,
    )
```

```python
import functools

import jax
import jax.numpy as jnp
from jax import lax
from jax.experimental import pallas as pl
from jax.experimental.pallas import tpu as pltpu
from jax.sharding import PartitionSpec as P

SIZE = 128
LOG2E = 1.4426950408889634
FACTOR = SIZE**-0.5
COST_CUT = 1
F32, BF16 = jnp.float32, jnp.bfloat16


def parts_of(x):
    high = x.astype(BF16)
    return high, (x - high.astype(F32)).astype(BF16)


def nt(a, b):
    return lax.dot_general(a, b, (((1,), (1,)), ((), ())), preferred_element_type=F32)


def nn(a, b):
    return lax.dot_general(a, b, (((1,), (0,)), ((), ())), preferred_element_type=F32)


def head_columns(head):
    return slice(head * SIZE, (head + 1) * SIZE)


def stacked(ref, first_head, pair):
    return jnp.concatenate([ref[:, head_columns(first_head + j)] for j in range(pair)], axis=0)


def load_rows(length, q_ref, g_ref, sub, pair):
    rows = q_ref.shape[0]
    q = stacked(q_ref, sub * pair, pair) * (FACTOR * LOG2E)
    token = lax.broadcasted_iota(jnp.int32, (pair, rows, SIZE), 1).reshape(pair * rows, SIZE)
    g = jnp.where(token < length, stacked(g_ref, sub * pair, pair), 0.0)
    return parts_of(q), parts_of(g)


def chunks_of(q_ref, pair):
    width = pair * q_ref.shape[0]
    for sub in range(q_ref.shape[1] // (pair * SIZE)):
        yield sub, slice(sub * width, (sub + 1) * width)


def keep_parts(refs, store):
    at = 0
    for ref in refs:
        high, low = parts_of(ref[...])
        store[at : at + ref.shape[0], :] = jnp.concatenate([high, low, high], axis=1)
        at += ref.shape[0]


def keep_turned(refs, store):
    at = 0
    for ref in refs:
        turned = ref[...].T
        high, low = parts_of(turned)
        store[:, at : at + ref.shape[0]] = jnp.concatenate([high, low], axis=0)
        at += ref.shape[0]


def masked(scores, length, rows, masked_rows):
    cut = scores.shape[0] - masked_rows
    slot = lax.broadcasted_iota(jnp.int32, (masked_rows, scores.shape[1]), 0)
    query = lax.broadcasted_iota(jnp.int32, (masked_rows, scores.shape[1]), 1) % rows
    visible = (slot <= query) & (slot < length)
    return jnp.concatenate([scores[:cut], jnp.where(visible, scores[cut:], -1e30)], axis=0)


def stats_rows(*rows):
    return jnp.concatenate(rows + (jnp.zeros((8 - len(rows), rows[0].shape[1]), F32),), axis=0)


def scores_and_dprobs(ka, va, rows):
    (qh, ql), (gh, gl) = rows
    scores = nt(ka[...], jnp.concatenate([qh, qh, ql], axis=1))
    dprobs = nt(va[...], jnp.concatenate([gh, gh, gl], axis=1))
    return scores, dprobs


def first_kernel(pair, key_count, count, masked_rows, length_ref, q_ref, g_ref, *refs):
    keys, values = refs[:key_count], refs[key_count:count]
    e_ref, dp_ref, stats_ref, ka, va = refs[count:]

    @pl.when(pl.program_id(0) == 0)
    def _():
        keep_parts(keys, ka)
        keep_parts(values, va)

    for sub, here in chunks_of(q_ref, pair):
        rows = load_rows(length_ref[0], q_ref, g_ref, sub, pair)
        scores, dprobs = scores_and_dprobs(ka, va, rows)
        if masked_rows:
            scores = masked(scores, length_ref[0], q_ref.shape[0], masked_rows)
        top = jnp.max(scores, axis=0, keepdims=True)
        e = jnp.exp2(scores - top)
        e_ref[:, here] = e
        dp_ref[:, here] = dprobs
        total = jnp.sum(e, axis=0, keepdims=True)
        weighted = jnp.sum(e * dprobs, axis=0, keepdims=True)
        stats_ref[:, here] = stats_rows(top, total, weighted)


def add_products(probs, ds, rows, kt, dk_sum, dv_sum):
    (qh, ql), (gh, gl) = rows
    ph, plow = parts_of(probs)
    sh, sl = parts_of(ds)
    gg = jnp.concatenate([gh, gl], axis=1)
    qq = jnp.concatenate([qh, ql], axis=1)
    dv_sum[...] += nn(jnp.concatenate([ph, plow], axis=1), jnp.concatenate([gg, gg], axis=0))
    dk_sum[...] += nn(jnp.concatenate([sh, sl], axis=1), jnp.concatenate([qq, qq], axis=0))
    both = nn(kt[...], sh)
    return ((both[:SIZE] + both[SIZE:] + nn(kt[:SIZE], sl)) * FACTOR).T


def store_query_grad(dq, before_ref, dq_ref, sub, pair):
    rows = dq_ref.shape[0]
    for j in range(pair):
        here = head_columns(sub * pair + j)
        part = dq[j * rows : (j + 1) * rows]
        dq_ref[:, here] = part if before_ref is None else part + before_ref[:, here]


def store_sums(refs, before, kept, scale):
    at = 0
    for j, ref in enumerate(refs):
        here = slice(at, at + ref.shape[0])
        part = (kept[here, :SIZE] + kept[here, SIZE:]) * scale
        ref[...] = part + before[j][...] if before else part
        at += ref.shape[0]


def start_sums(dk_sum, dv_sum):
    dk_sum[...] = jnp.zeros_like(dk_sum)
    dv_sum[...] = jnp.zeros_like(dv_sum)


def middle_kernel(pair, value_count, length_ref, q_ref, g_ref, stats_a, stats_b, k_ref, *refs):
    values = refs[:value_count]
    dq_ref, final_ref, dk_ref, dv_ref, ka, va, kt, dk_sum, dv_sum = refs[value_count:]

    @pl.when(pl.program_id(0) == 0)
    def _():
        keep_parts([k_ref], ka)
        keep_parts(values, va)
        keep_turned([k_ref], kt)
        start_sums(dk_sum, dv_sum)

    for sub, here in chunks_of(q_ref, pair):
        rows = load_rows(length_ref[0], q_ref, g_ref, sub, pair)
        scores, dprobs = scores_and_dprobs(ka, va, rows)
        top_a, top_b = stats_a[0:1, here], stats_b[0:1, here]
        top = jnp.maximum(jnp.maximum(top_a, top_b), jnp.max(scores, axis=0, keepdims=True))
        e = jnp.exp2(scores - top)
        fade_a, fade_b = jnp.exp2(top_a - top), jnp.exp2(top_b - top)
        total = stats_a[1:2, here] * fade_a + stats_b[1:2, here] * fade_b
        total = total + jnp.sum(e, axis=0, keepdims=True)
        weighted = stats_a[2:3, here] * fade_a + stats_b[2:3, here] * fade_b
        weighted = weighted + jnp.sum(e * dprobs, axis=0, keepdims=True)
        inverse = 1.0 / total
        dsum = weighted * inverse
        final_ref[:, here] = stats_rows(fade_a * inverse, fade_b * inverse, dsum)
        probs = e * inverse
        ds = probs * (dprobs - dsum)
        dq = add_products(probs, ds, rows, kt, dk_sum, dv_sum)
        store_query_grad(dq, None, dq_ref, sub, pair)

    @pl.when(pl.program_id(0) == pl.num_programs(0) - 1)
    def _():
        store_sums([dk_ref], [], dk_sum, 1.0 / LOG2E)
        store_sums([dv_ref], [], dv_sum, 1.0)


def last_kernel(
    pair, count, before_count, scale_row, pieces,
    length_ref, place_ref, q_ref, g_ref, before_ref, e_ref, dp_ref, final_ref, *refs,
):
    keys, refs = refs[:count], refs[count:]
    before_dk, before_dv = refs[:before_count], refs[before_count : 2 * before_count]
    refs = refs[2 * before_count :]
    dq_refs, refs = refs[:pieces], refs[pieces:]
    dk_refs, dv_refs = refs[:count], refs[count : 2 * count]
    kt, dk_sum, dv_sum, *held = refs[2 * count :]
    dq_ref = held[0] if held else dq_refs[0]

    @pl.when(pl.program_id(0) == 0)
    def _():
        keep_turned(keys, kt)
        start_sums(dk_sum, dv_sum)

    for sub, here in chunks_of(q_ref, pair):
        rows = load_rows(length_ref[0], q_ref, g_ref, sub, pair)
        probs = e_ref[:, here] * final_ref[scale_row : scale_row + 1, here]
        ds = probs * (dp_ref[:, here] - final_ref[2:3, here])
        dq = add_products(probs, ds, rows, kt, dk_sum, dv_sum)
        store_query_grad(dq, before_ref, dq_ref, sub, pair)
    if held:
        size = dq_ref.shape[0] // pieces
        for j in range(pieces):
            at = pl.multiple_of((place_ref[0] ^ j) * size, size)
            dq_refs[j][...] = dq_ref[pl.ds(at, size), :]

    @pl.when(pl.program_id(0) == pl.num_programs(0) - 1)
    def _():
        store_sums(dk_refs, before_dk, dk_sum, 1.0 / LOG2E)
        store_sums(dv_refs, before_dv, dv_sum, 1.0)


SMEM = pl.BlockSpec(memory_space=pltpu.SMEM)


def shape_of(*dims):
    return jax.ShapeDtypeStruct(dims, F32)


def by_columns(rows, width, first=0):
    return pl.BlockSpec((rows, width), lambda i: (0, i + first))


def whole(arrays):
    return [pl.BlockSpec(a.shape, lambda i: (0, 0)) for a in arrays]


def like(arrays):
    return [shape_of(*a.shape) for a in arrays]


def settings(products, rows, width, total, moved):
    return dict(
        compiler_params=pltpu.CompilerParams(vmem_limit_bytes=24 * 2**20),
        cost_estimate=pl.CostEstimate(
            flops=2 * products * 4 * rows * width * total // COST_CUT,
            bytes_accessed=moved // COST_CUT,
            transcendentals=0,
        ),
    )


def first_pass(lengths, queries, out_grad, keys, values, masked_rows, name, pair=8, step=8):
    rows, width = queries.shape
    total = sum(k.shape[0] for k in keys)
    slots = rows * width // SIZE
    per_head, per_slot = by_columns(rows, step * SIZE), by_columns(total, step * rows)
    return pl.pallas_call(
        functools.partial(first_kernel, pair, len(keys), len(keys) + len(values), masked_rows),
        grid=(width // (step * SIZE),),
        in_specs=[SMEM, per_head, per_head] + whole(keys) + whole(values),
        out_specs=[per_slot, per_slot, by_columns(8, step * rows)],
        out_shape=[shape_of(total, slots)] * 2 + [shape_of(8, slots)],
        scratch_shapes=[pltpu.VMEM((total, 3 * SIZE), BF16)] * 2,
        name=name,
        **settings(2, rows, width, total, 8 * total * slots),
    )(lengths, queries, out_grad, *keys, *values)


def middle_pass(lengths, queries, out_grad, stats_a, stats_b, key_block, values, pair=8, step=16):
    rows, width = queries.shape
    total = key_block.shape[0]
    slots = rows * width // SIZE
    per_head, stats = by_columns(rows, step * SIZE), by_columns(8, step * rows)
    return pl.pallas_call(
        functools.partial(middle_kernel, pair, len(values)),
        grid=(width // (step * SIZE),),
        in_specs=[SMEM, per_head, per_head, stats, stats] + whole([key_block]) + whole(values),
        out_specs=[per_head, stats] + whole([key_block, key_block]),
        out_shape=[shape_of(rows, width), shape_of(8, slots)] + like([key_block, key_block]),
        scratch_shapes=[pltpu.VMEM((total, 3 * SIZE), BF16)] * 2
        + [pltpu.VMEM((2 * SIZE, total), BF16)]
        + [pltpu.VMEM((total, 2 * SIZE), F32)] * 2,
        name="middle_pass",
        **settings(5, rows, width, total, 5_000_000),
    )(lengths, queries, out_grad, stats_a, stats_b, key_block, *values)


def last_pass(
    lengths, queries, out_grad, place, before, e, dp, final, scale_row, keys, name,
    first=0, heads=16, before_sums=(), pieces=1, pair=8, step=8,
):
    rows = queries.shape[0]
    total = sum(k.shape[0] for k in keys)
    start = first // step
    per_head = by_columns(rows, step * SIZE, start)
    per_slot = by_columns(total, step * rows, start)
    stats = by_columns(8, step * rows, start)
    return pl.pallas_call(
        functools.partial(last_kernel, pair, len(keys), len(before_sums) // 2, scale_row, pieces),
        grid=(heads // step,),
        in_specs=[SMEM, SMEM, per_head, per_head, per_head, per_slot, per_slot, stats]
        + whole(keys) + whole(before_sums),
        out_specs=[by_columns(rows // pieces, step * SIZE)] * pieces + whole(keys) + whole(keys),
        out_shape=[shape_of(rows // pieces, heads * SIZE)] * pieces + like(keys) + like(keys),
        scratch_shapes=[pltpu.VMEM((2 * SIZE, total), BF16)]
        + [pltpu.VMEM((total, 2 * SIZE), F32)] * 2
        + [pltpu.VMEM((rows, step * SIZE), F32)] * (pieces > 1),
        name=name,
        **settings(3, rows, heads * SIZE, total, 8 * total * heads * rows),
    )(lengths, place, queries, out_grad, before, e, dp, final, *keys, *before_sums)


def sum_kernel(odd_ref, own_ref, near_ref, far_ref, out_ref):
    near = jnp.where(odd_ref[0] == 1, near_ref[...], 0.0)
    out_ref[...] = own_ref[...] + near + far_ref[...]


def gather_kernel(count, place_ref, *refs):
    out_ref, half = refs[-1], refs[0].shape[1]
    for j in range(count):
        for k in range(2):
            at = pl.multiple_of(((place_ref[0] ^ j) * 2 + k) * half, half)
            out_ref[:, pl.ds(at, half)] = refs[2 * j + k][...]


def sum_pass(odd, own, near, far, name):
    blocks = whole([own, near, far])
    return pl.pallas_call(
        sum_kernel,
        grid=(1,),
        in_specs=[SMEM] + blocks,
        out_specs=blocks[0],
        out_shape=shape_of(*own.shape),
        compiler_params=pltpu.CompilerParams(vmem_limit_bytes=8 * 2**20),
        name=name,
    )(odd, own, near, far)


def gather_pass(place, parts):
    rows, half = parts[0].shape
    return pl.pallas_call(
        functools.partial(gather_kernel, len(parts) // 2),
        grid=(1,),
        in_specs=[SMEM] + whole(parts),
        out_specs=pl.BlockSpec((rows, len(parts) * half), lambda i: (0, 0)),
        out_shape=shape_of(rows, len(parts) * half),
        compiler_params=pltpu.CompilerParams(vmem_limit_bytes=8 * 2**20),
        name="gather_queries",
    )(place, *parts)


def per_device(
    queries, prefix_keys, prefix_value_rows, response_keys, response_values, out_grad, lengths
):
    count = lax.axis_size("seq")
    head_devices = lax.axis_size("head")
    even = lax.axis_index("seq") % 2 == 0
    odd = (lax.axis_index("seq") % 2).astype(jnp.int32).reshape(1)
    place = lax.axis_index("head").astype(jnp.int32).reshape(1)
    rows, width = queries.shape
    heads = width // SIZE
    half = prefix_keys.shape[0] // 2

    def from_two_on(block):
        return lax.ppermute(block, "seq", [((i + 2) % count, i) for i in range(count)])

    def to_two_on(block):
        return lax.ppermute(block, "seq", [(i, (i + 2) % count) for i in range(count)])

    def swapped(block):
        return lax.ppermute(block, "seq", [(i, i ^ 1) for i in range(count)])

    def exchanged(block, bits):
        return lax.ppermute(block, "head", [(i, i ^ bits) for i in range(head_devices)])

    def split_grads(grads):
        return grads[:head_devices], grads[head_devices:]

    args = (lengths, queries, out_grad)
    value_parts = [prefix_value_rows[:half], prefix_value_rows[half:]]
    far_k = from_two_on(prefix_keys)
    far_v = [from_two_on(part) for part in value_parts]

    own_keys, own_values = [prefix_keys, response_keys], [prefix_value_rows, response_values]
    own_e, own_dp, own_stats = first_pass(*args, own_keys, own_values, rows, "own_scores")
    own_stats, far_k = lax.optimization_barrier((own_stats, far_k))
    near_k = swapped(jnp.where(even, far_k, prefix_keys))
    near_v = []
    for j in range(2):
        own_stats, far_v[j] = lax.optimization_barrier((own_stats, far_v[j]))
        chosen = jnp.where(even, far_v[j], value_parts[j])
        near_v.append(swapped(chosen))
    own_stats, far_k, chosen = lax.optimization_barrier((own_stats, far_k, chosen))
    far_e, far_dp, far_stats = first_pass(*args, [far_k], far_v, 0, "far_scores")
    near_dq, final, near_dk, near_dv = middle_pass(*args, own_stats, far_stats, near_k, near_v)

    from_near_dv, from_near_dk = swapped(near_dv), swapped(near_dk)
    far_dq, far_dk, far_dv = last_pass(
        *args, place, near_dq, far_e, far_dp, final, 1, [far_k], "far_grads"
    )
    to_far_dv = far_dv + jnp.where(even, from_near_dv, 0.0)
    from_far_dv = to_two_on(to_far_dv)
    far_dq, to_far_dv = lax.optimization_barrier((far_dq, to_far_dv))
    dq_a, sums = split_grads(last_pass(
        *args, place, far_dq, own_e, own_dp, final, 0, own_keys, "own_grads_a",
        first=0, heads=heads // 2, pieces=head_devices,
    ))
    got_a = [dq_a[0]] + [exchanged(dq_a[j], j) for j in range(1, head_devices)]
    to_far_dk = far_dk + jnp.where(even, from_near_dk, 0.0)
    sums, to_far_dk, far_dq = lax.optimization_barrier((sums, to_far_dk, far_dq))
    from_far_dk = to_two_on(to_far_dk)
    dq_b, (own_dk, resp_dk, own_dv, resp_dv) = split_grads(last_pass(
        *args, place, far_dq, own_e, own_dp, final, 0, own_keys, "own_grads_b",
        first=heads // 2, heads=heads // 2, before_sums=sums, pieces=head_devices,
    ))
    got_a, dq_b = lax.optimization_barrier((got_a, dq_b))
    got_b = [dq_b[0]] + [exchanged(dq_b[j], j) for j in range(1, head_devices)]
    grad_v = sum_pass(odd, own_dv, from_near_dv, from_far_dv, "sum_values")
    grad_k = sum_pass(odd, own_dk, from_near_dk, from_far_dk, "sum_keys")
    got_b, grad_k, grad_v = lax.optimization_barrier((got_b, grad_k, grad_v))
    grad_queries = gather_pass(place, [x for pair in zip(got_a, got_b) for x in pair])
    return (grad_queries, grad_k, grad_v, resp_dk, resp_dv)


def solution(mesh):
    placed = (P("seq", "head"),) * 6 + (P("seq"),)
    return jax.shard_map(
        per_device,
        mesh=mesh,
        in_specs=placed,
        out_specs=(P(("seq", "head"), None),) + (P("seq", "head"),) * 4,
        check_vma=False,
    )
```

```python
import functools

import jax
import jax.numpy as jnp
from jax import lax
from jax.experimental import pallas as pl
from jax.experimental.pallas import tpu as pltpu
from jax.sharding import PartitionSpec as P

SIZE = 128
LOG2E = 1.4426950408889634
FACTOR = SIZE**-0.5
COST_CUT = 1
F32, BF16 = jnp.float32, jnp.bfloat16


def parts_of(x):
    high = x.astype(BF16)
    return high, (x - high.astype(F32)).astype(BF16)


def nt(a, b):
    return lax.dot_general(a, b, (((1,), (1,)), ((), ())), preferred_element_type=F32)


def nn(a, b):
    return lax.dot_general(a, b, (((1,), (0,)), ((), ())), preferred_element_type=F32)


def head_columns(head):
    return slice(head * SIZE, (head + 1) * SIZE)


def stacked(ref, first_head, pair):
    return jnp.concatenate([ref[:, head_columns(first_head + j)] for j in range(pair)], axis=0)


def load_rows(length, q_ref, g_ref, sub, pair):
    rows = q_ref.shape[0]
    q = stacked(q_ref, sub * pair, pair) * (FACTOR * LOG2E)
    token = lax.broadcasted_iota(jnp.int32, (pair, rows, SIZE), 1).reshape(pair * rows, SIZE)
    g = jnp.where(token < length, stacked(g_ref, sub * pair, pair), 0.0)
    return parts_of(q), parts_of(g)


def chunks_of(q_ref, pair):
    width = pair * q_ref.shape[0]
    for sub in range(q_ref.shape[1] // (pair * SIZE)):
        yield sub, slice(sub * width, (sub + 1) * width)


def keep_parts(refs, store):
    at = 0
    for ref in refs:
        high, low = parts_of(ref[...])
        store[at : at + ref.shape[0], :] = jnp.concatenate([high, low, high], axis=1)
        at += ref.shape[0]


def keep_turned(refs, store):
    at = 0
    for ref in refs:
        turned = ref[...].T
        high, low = parts_of(turned)
        store[:, at : at + ref.shape[0]] = jnp.concatenate([high, low], axis=0)
        at += ref.shape[0]


def masked(scores, length, rows, masked_rows):
    cut = scores.shape[0] - masked_rows
    slot = lax.broadcasted_iota(jnp.int32, (masked_rows, scores.shape[1]), 0)
    query = lax.broadcasted_iota(jnp.int32, (masked_rows, scores.shape[1]), 1) % rows
    visible = (slot <= query) & (slot < length)
    return jnp.concatenate([scores[:cut], jnp.where(visible, scores[cut:], -1e30)], axis=0)


def stats_rows(*rows):
    return jnp.concatenate(rows + (jnp.zeros((8 - len(rows), rows[0].shape[1]), F32),), axis=0)


def scores_and_dprobs(ka, va, rows):
    (qh, ql), (gh, gl) = rows
    scores = nt(ka[...], jnp.concatenate([qh, qh, ql], axis=1))
    dprobs = nt(va[...], jnp.concatenate([gh, gh, gl], axis=1))
    return scores, dprobs


def first_kernel(pair, key_count, count, masked_rows, length_ref, q_ref, g_ref, *refs):
    keys, values = refs[:key_count], refs[key_count:count]
    e_ref, dp_ref, stats_ref, ka, va = refs[count:]

    @pl.when(pl.program_id(0) == 0)
    def _():
        keep_parts(keys, ka)
        keep_parts(values, va)

    for sub, here in chunks_of(q_ref, pair):
        rows = load_rows(length_ref[0], q_ref, g_ref, sub, pair)
        scores, dprobs = scores_and_dprobs(ka, va, rows)
        if masked_rows:
            scores = masked(scores, length_ref[0], q_ref.shape[0], masked_rows)
        top = jnp.max(scores, axis=0, keepdims=True)
        e = jnp.exp2(scores - top)
        e_ref[:, here] = e
        dp_ref[:, here] = dprobs
        total = jnp.sum(e, axis=0, keepdims=True)
        weighted = jnp.sum(e * dprobs, axis=0, keepdims=True)
        stats_ref[:, here] = stats_rows(top, total, weighted)


def add_products(probs, ds, rows, kt, dk_sum, dv_sum):
    (qh, ql), (gh, gl) = rows
    ph, plow = parts_of(probs)
    sh, sl = parts_of(ds)
    gg = jnp.concatenate([gh, gl], axis=1)
    qq = jnp.concatenate([qh, ql], axis=1)
    dv_sum[...] += nn(jnp.concatenate([ph, plow], axis=1), jnp.concatenate([gg, gg], axis=0))
    dk_sum[...] += nn(jnp.concatenate([sh, sl], axis=1), jnp.concatenate([qq, qq], axis=0))
    both = nn(kt[...], sh)
    return ((both[:SIZE] + both[SIZE:] + nn(kt[:SIZE], sl)) * FACTOR).T


def store_query_grad(dq, before_ref, dq_ref, sub, pair):
    rows = dq_ref.shape[0]
    for j in range(pair):
        here = head_columns(sub * pair + j)
        part = dq[j * rows : (j + 1) * rows]
        dq_ref[:, here] = part if before_ref is None else part + before_ref[:, here]


def store_sums(refs, before, kept, scale):
    at = 0
    for j, ref in enumerate(refs):
        here = slice(at, at + ref.shape[0])
        part = (kept[here, :SIZE] + kept[here, SIZE:]) * scale
        ref[...] = part + before[j][...] if before else part
        at += ref.shape[0]


def start_sums(dk_sum, dv_sum):
    dk_sum[...] = jnp.zeros_like(dk_sum)
    dv_sum[...] = jnp.zeros_like(dv_sum)


def middle_kernel(pair, value_count, length_ref, q_ref, g_ref, stats_a, stats_b, k_ref, *refs):
    values = refs[:value_count]
    dq_ref, final_ref, dk_ref, dv_ref, ka, va, kt, dk_sum, dv_sum = refs[value_count:]

    @pl.when(pl.program_id(0) == 0)
    def _():
        keep_parts([k_ref], ka)
        keep_parts(values, va)
        keep_turned([k_ref], kt)
        start_sums(dk_sum, dv_sum)

    for sub, here in chunks_of(q_ref, pair):
        rows = load_rows(length_ref[0], q_ref, g_ref, sub, pair)
        scores, dprobs = scores_and_dprobs(ka, va, rows)
        top_a, top_b = stats_a[0:1, here], stats_b[0:1, here]
        top = jnp.maximum(jnp.maximum(top_a, top_b), jnp.max(scores, axis=0, keepdims=True))
        e = jnp.exp2(scores - top)
        fade_a, fade_b = jnp.exp2(top_a - top), jnp.exp2(top_b - top)
        total = stats_a[1:2, here] * fade_a + stats_b[1:2, here] * fade_b
        total = total + jnp.sum(e, axis=0, keepdims=True)
        weighted = stats_a[2:3, here] * fade_a + stats_b[2:3, here] * fade_b
        weighted = weighted + jnp.sum(e * dprobs, axis=0, keepdims=True)
        inverse = 1.0 / total
        dsum = weighted * inverse
        final_ref[:, here] = stats_rows(fade_a * inverse, fade_b * inverse, dsum)
        probs = e * inverse
        ds = probs * (dprobs - dsum)
        dq = add_products(probs, ds, rows, kt, dk_sum, dv_sum)
        store_query_grad(dq, None, dq_ref, sub, pair)

    @pl.when(pl.program_id(0) == pl.num_programs(0) - 1)
    def _():
        store_sums([dk_ref], [], dk_sum, 1.0 / LOG2E)
        store_sums([dv_ref], [], dv_sum, 1.0)


def last_kernel(
    pair, count, before_count, scale_row, pieces,
    length_ref, place_ref, q_ref, g_ref, before_ref, e_ref, dp_ref, final_ref, *refs,
):
    keys, refs = refs[:count], refs[count:]
    before_dk, before_dv = refs[:before_count], refs[before_count : 2 * before_count]
    refs = refs[2 * before_count :]
    dq_refs, refs = refs[:pieces], refs[pieces:]
    dk_refs, dv_refs = refs[:count], refs[count : 2 * count]
    kt, dk_sum, dv_sum, *held = refs[2 * count :]
    dq_ref = held[0] if held else dq_refs[0]

    @pl.when(pl.program_id(0) == 0)
    def _():
        keep_turned(keys, kt)
        start_sums(dk_sum, dv_sum)

    for sub, here in chunks_of(q_ref, pair):
        rows = load_rows(length_ref[0], q_ref, g_ref, sub, pair)
        probs = e_ref[:, here] * final_ref[scale_row : scale_row + 1, here]
        ds = probs * (dp_ref[:, here] - final_ref[2:3, here])
        dq = add_products(probs, ds, rows, kt, dk_sum, dv_sum)
        store_query_grad(dq, before_ref, dq_ref, sub, pair)
    if held:
        size = dq_ref.shape[0] // pieces
        for j in range(pieces):
            at = pl.multiple_of((place_ref[0] ^ j) * size, size)
            dq_refs[j][...] = dq_ref[pl.ds(at, size), :]

    @pl.when(pl.program_id(0) == pl.num_programs(0) - 1)
    def _():
        store_sums(dk_refs, before_dk, dk_sum, 1.0 / LOG2E)
        store_sums(dv_refs, before_dv, dv_sum, 1.0)


SMEM = pl.BlockSpec(memory_space=pltpu.SMEM)


def shape_of(*dims):
    return jax.ShapeDtypeStruct(dims, F32)


def by_columns(rows, width, first=0):
    return pl.BlockSpec((rows, width), lambda i: (0, i + first))


def whole(arrays):
    return [pl.BlockSpec(a.shape, lambda i: (0, 0)) for a in arrays]


def like(arrays):
    return [shape_of(*a.shape) for a in arrays]


def settings(products, rows, width, total, moved):
    return dict(
        compiler_params=pltpu.CompilerParams(vmem_limit_bytes=24 * 2**20),
        cost_estimate=pl.CostEstimate(
            flops=2 * products * 4 * rows * width * total // COST_CUT,
            bytes_accessed=moved // COST_CUT,
            transcendentals=0,
        ),
    )


def first_pass(lengths, queries, out_grad, keys, values, masked_rows, name, pair=8, step=8):
    rows, width = queries.shape
    total = sum(k.shape[0] for k in keys)
    slots = rows * width // SIZE
    per_head, per_slot = by_columns(rows, step * SIZE), by_columns(total, step * rows)
    return pl.pallas_call(
        functools.partial(first_kernel, pair, len(keys), len(keys) + len(values), masked_rows),
        grid=(width // (step * SIZE),),
        in_specs=[SMEM, per_head, per_head] + whole(keys) + whole(values),
        out_specs=[per_slot, per_slot, by_columns(8, step * rows)],
        out_shape=[shape_of(total, slots)] * 2 + [shape_of(8, slots)],
        scratch_shapes=[pltpu.VMEM((total, 3 * SIZE), BF16)] * 2,
        name=name,
        **settings(2, rows, width, total, 8 * total * slots),
    )(lengths, queries, out_grad, *keys, *values)


def middle_pass(lengths, queries, out_grad, stats_a, stats_b, key_block, values, pair=16, step=16):
    rows, width = queries.shape
    total = key_block.shape[0]
    slots = rows * width // SIZE
    per_head, stats = by_columns(rows, step * SIZE), by_columns(8, step * rows)
    return pl.pallas_call(
        functools.partial(middle_kernel, pair, len(values)),
        grid=(width // (step * SIZE),),
        in_specs=[SMEM, per_head, per_head, stats, stats] + whole([key_block]) + whole(values),
        out_specs=[per_head, stats] + whole([key_block, key_block]),
        out_shape=[shape_of(rows, width), shape_of(8, slots)] + like([key_block, key_block]),
        scratch_shapes=[pltpu.VMEM((total, 3 * SIZE), BF16)] * 2
        + [pltpu.VMEM((2 * SIZE, total), BF16)]
        + [pltpu.VMEM((total, 2 * SIZE), F32)] * 2,
        name="middle_pass",
        **settings(5, rows, width, total, 5_000_000),
    )(lengths, queries, out_grad, stats_a, stats_b, key_block, *values)


def last_pass(
    lengths, queries, out_grad, place, before, e, dp, final, scale_row, keys, name,
    first=0, heads=16, before_sums=(), pieces=1, pair=8, step=8,
):
    rows = queries.shape[0]
    total = sum(k.shape[0] for k in keys)
    start = first // step
    per_head = by_columns(rows, step * SIZE, start)
    per_slot = by_columns(total, step * rows, start)
    stats = by_columns(8, step * rows, start)
    return pl.pallas_call(
        functools.partial(last_kernel, pair, len(keys), len(before_sums) // 2, scale_row, pieces),
        grid=(heads // step,),
        in_specs=[SMEM, SMEM, per_head, per_head, per_head, per_slot, per_slot, stats]
        + whole(keys) + whole(before_sums),
        out_specs=[by_columns(rows // pieces, step * SIZE)] * pieces + whole(keys) + whole(keys),
        out_shape=[shape_of(rows // pieces, heads * SIZE)] * pieces + like(keys) + like(keys),
        scratch_shapes=[pltpu.VMEM((2 * SIZE, total), BF16)]
        + [pltpu.VMEM((total, 2 * SIZE), F32)] * 2
        + [pltpu.VMEM((rows, step * SIZE), F32)] * (pieces > 1),
        name=name,
        **settings(3, rows, heads * SIZE, total, 8 * total * heads * rows),
    )(lengths, place, queries, out_grad, before, e, dp, final, *keys, *before_sums)


def sum_kernel(odd_ref, own_ref, near_ref, far_ref, out_ref):
    near = jnp.where(odd_ref[0] == 1, near_ref[...], 0.0)
    out_ref[...] = own_ref[...] + near + far_ref[...]


def gather_kernel(count, place_ref, *refs):
    out_ref, half = refs[-1], refs[0].shape[1]
    for j in range(count):
        for k in range(2):
            at = pl.multiple_of(((place_ref[0] ^ j) * 2 + k) * half, half)
            out_ref[:, pl.ds(at, half)] = refs[2 * j + k][...]


def sum_pass(odd, own, near, far, name):
    blocks = whole([own, near, far])
    return pl.pallas_call(
        sum_kernel,
        grid=(1,),
        in_specs=[SMEM] + blocks,
        out_specs=blocks[0],
        out_shape=shape_of(*own.shape),
        compiler_params=pltpu.CompilerParams(vmem_limit_bytes=8 * 2**20),
        name=name,
    )(odd, own, near, far)


def gather_pass(place, parts):
    rows, half = parts[0].shape
    return pl.pallas_call(
        functools.partial(gather_kernel, len(parts) // 2),
        grid=(1,),
        in_specs=[SMEM] + whole(parts),
        out_specs=pl.BlockSpec((rows, len(parts) * half), lambda i: (0, 0)),
        out_shape=shape_of(rows, len(parts) * half),
        compiler_params=pltpu.CompilerParams(vmem_limit_bytes=8 * 2**20),
        name="gather_queries",
    )(place, *parts)


def per_device(
    queries, prefix_keys, prefix_value_rows, response_keys, response_values, out_grad, lengths
):
    count = lax.axis_size("seq")
    head_devices = lax.axis_size("head")
    even = lax.axis_index("seq") % 2 == 0
    odd = (lax.axis_index("seq") % 2).astype(jnp.int32).reshape(1)
    place = lax.axis_index("head").astype(jnp.int32).reshape(1)
    rows, width = queries.shape
    heads = width // SIZE
    half = prefix_keys.shape[0] // 2

    def from_two_on(block):
        return lax.ppermute(block, "seq", [((i + 2) % count, i) for i in range(count)])

    def to_two_on(block):
        return lax.ppermute(block, "seq", [(i, (i + 2) % count) for i in range(count)])

    def swapped(block):
        return lax.ppermute(block, "seq", [(i, i ^ 1) for i in range(count)])

    def exchanged(block, bits):
        return lax.ppermute(block, "head", [(i, i ^ bits) for i in range(head_devices)])

    def split_grads(grads):
        return grads[:head_devices], grads[head_devices:]

    args = (lengths, queries, out_grad)
    value_parts = [prefix_value_rows[:half], prefix_value_rows[half:]]
    far_k = from_two_on(prefix_keys)
    far_v = [from_two_on(part) for part in value_parts]

    own_keys, own_values = [prefix_keys, response_keys], [prefix_value_rows, response_values]
    own_e, own_dp, own_stats = first_pass(*args, own_keys, own_values, rows, "own_scores")
    own_stats, far_k = lax.optimization_barrier((own_stats, far_k))
    near_k = swapped(jnp.where(even, far_k, prefix_keys))
    near_v = []
    for j in range(2):
        own_stats, far_v[j] = lax.optimization_barrier((own_stats, far_v[j]))
        chosen = jnp.where(even, far_v[j], value_parts[j])
        near_v.append(swapped(chosen))
    own_stats, far_k, chosen = lax.optimization_barrier((own_stats, far_k, chosen))
    far_e, far_dp, far_stats = first_pass(*args, [far_k], far_v, 0, "far_scores")
    near_dq, final, near_dk, near_dv = middle_pass(*args, own_stats, far_stats, near_k, near_v)

    from_near_dv, from_near_dk = swapped(near_dv), swapped(near_dk)
    far_dq, far_dk, far_dv = last_pass(
        *args, place, near_dq, far_e, far_dp, final, 1, [far_k], "far_grads"
    )
    to_far_dv = far_dv + jnp.where(even, from_near_dv, 0.0)
    from_far_dv = to_two_on(to_far_dv)
    far_dq, to_far_dv = lax.optimization_barrier((far_dq, to_far_dv))
    dq_a, sums = split_grads(last_pass(
        *args, place, far_dq, own_e, own_dp, final, 0, own_keys, "own_grads_a",
        first=0, heads=heads // 2, pieces=head_devices,
    ))
    got_a = [dq_a[0]] + [exchanged(dq_a[j], j) for j in range(1, head_devices)]
    to_far_dk = far_dk + jnp.where(even, from_near_dk, 0.0)
    sums, to_far_dk, far_dq = lax.optimization_barrier((sums, to_far_dk, far_dq))
    from_far_dk = to_two_on(to_far_dk)
    dq_b, (own_dk, resp_dk, own_dv, resp_dv) = split_grads(last_pass(
        *args, place, far_dq, own_e, own_dp, final, 0, own_keys, "own_grads_b",
        first=heads // 2, heads=heads // 2, before_sums=sums, pieces=head_devices,
    ))
    got_a, dq_b = lax.optimization_barrier((got_a, dq_b))
    got_b = [dq_b[0]] + [exchanged(dq_b[j], j) for j in range(1, head_devices)]
    grad_v = sum_pass(odd, own_dv, from_near_dv, from_far_dv, "sum_values")
    grad_k = sum_pass(odd, own_dk, from_near_dk, from_far_dk, "sum_keys")
    got_b, grad_k, grad_v = lax.optimization_barrier((got_b, grad_k, grad_v))
    grad_queries = gather_pass(place, [x for pair in zip(got_a, got_b) for x in pair])
    return (grad_queries, grad_k, grad_v, resp_dk, resp_dv)


def solution(mesh):
    placed = (P("seq", "head"),) * 6 + (P("seq"),)
    return jax.shard_map(
        per_device,
        mesh=mesh,
        in_specs=placed,
        out_specs=(P(("seq", "head"), None),) + (P("seq", "head"),) * 4,
        check_vma=False,
    )
```
